512 devices in a mesh: replica: 16 (over x, z_hi), fsdp: 32 (over z_lo, y, core).
Axes of the slice: x: 4, y: 8, z: 8 (z_hi: 4, z_lo: 2; z = z_hi * 2 + z_lo), core: 2. Of those that a mesh axis runs over, the one named last changes fastest.
Arguments:
- anchor: float32 [3328, 3328], P('fsdp', 'replica'), may hold values from -6 to 6
- prev_delta: bfloat16 [16, 3328, 3328], P('replica', 'fsdp'), may hold values from -4 to 4
- momentum: float32 [3328, 3328], P('fsdp', 'replica'), may hold values from -2 to 2
- pool: bfloat16 [16, 1024, 3328], P('replica', 'fsdp'), may hold values from -6 to 6
- ids: int32 [16, 2, 1024], P('replica', None, 'fsdp'), may hold values from 0 to 31
- cotangent: bfloat16 [16, 2, 3328, 1024], P('replica', None, 'fsdp'), may hold values from -6 to 6
Outputs:
- new_delta: bfloat16 [16, 3328, 3328], P('replica', 'fsdp')
- new_anchor: float32 [3328, 3328], P('fsdp', 'replica')
- new_momentum: float32 [3328, 3328], P('fsdp', 'replica')
The draws below stay inside these ranges and needn't reach their ends.
All inputs are finite; a program needn't handle non-finite values.
Results may differ from the reference program's by a relative error of at most 0.0062.
Values may be sent and summed in bfloat16 or wider, within the bound.
No kernel may reach another device: no remote copies, remote signals or barrier semaphores. Data moves between devices by JAX's collectives and lax.ppermute only.
A program may use at most 64 MiB of HBM per device.

```python
import math
import jax
import jax.numpy as jnp
from jax import lax

D = 3328
HW = 3328
STEPS = 2
TOK_DEV = 32
POOL_DEV = 32
ISLANDS = 16
TOK_ISL = 1024
ROWS = 1024
N_REPLICA = 16
N_FSDP = 32


def level_fields(key, slope_log, row_spread):
    key_rows, key_cols, key_rough_rows, key_rough_cols, key_common = jax.random.split(key, 5)
    row_block = jax.random.uniform(key_rows, (16,), jnp.float32, -1.0, 1.0)
    col_block = jax.random.uniform(key_cols, (16,), jnp.float32, -1.0, 1.0)
    row_index = jnp.arange(HW, dtype=jnp.int32)
    col_index = jnp.arange(D, dtype=jnp.int32)
    row_log = row_spread * row_block[row_index * 16 // HW]
    row_log = row_log + jax.random.uniform(key_rough_rows, (HW,), jnp.float32, -0.35, 0.35)
    col_place = (2.0 * col_index.astype(jnp.float32) + 1.0) / D - 1.0
    col_log = slope_log * col_place + 0.4 * col_block[col_index * 16 // D]
    col_log = col_log + jax.random.uniform(key_rough_cols, (D,), jnp.float32, -0.35, 0.35)
    common = jax.random.normal(key_common, (HW, D), jnp.float32)
    return (jnp.exp(row_log), jnp.exp(col_log), common)


def draw_prev_delta(key, part):
    slope_log, row_spread, common_share, own_share = (0.58, 0.58, 0.25, 0.15)
    row_level, col_level, common = level_fields(key, slope_log, row_spread)
    key = jax.random.fold_in(key, 21)
    key_own, key_pair = jax.random.split(key)
    own_part = jax.random.normal(key_own, (ISLANDS, HW, D), jnp.float32)
    pairing = jax.random.permutation(key_pair, ISLANDS).astype(jnp.int32)
    col_group = jnp.arange(D, dtype=jnp.int32) * ISLANDS // D
    spike_gain = jnp.where(col_group[None, :] == pairing[:, None], 6.0, 1.0).astype(jnp.float32)
    shared_part = row_level[:, None] * col_level[None, :] * common_share * common
    values = shared_part[None] + own_share * row_level[None, :, None] * spike_gain[:, None, :] * own_part
    return jnp.clip(values, -4.0, 4.0).astype(jnp.bfloat16)


def draw_momentum(key, part):
    slope_log, row_spread, common_share = (0.58, 0.58, 0.08)
    row_level, col_level, common = level_fields(key, slope_log, row_spread)
    key = jax.random.fold_in(key, 22)
    own_part = jax.random.normal(key, (HW, D), jnp.float32)
    values = row_level[:, None] * (common_share * col_level[None, :] * common + 0.05 * own_part)
    return jnp.clip(values, -2.0, 2.0)


def with_ends(entries, stream_key, least, largest):
    place = [jax.random.randint(jax.random.fold_in(stream_key, axis), (), 0, length) for axis, length in enumerate(entries.shape)]
    longest = entries.shape.index(max(entries.shape))
    next_to = place[:longest] + [(place[longest] + 1) % entries.shape[longest]] + place[longest + 1:]
    return entries.at[tuple(place)].set(least).at[tuple(next_to)].set(largest)


def shard_levels(key, dims, cuts, low, top_value):
    gain = 1.0
    for dim, shards_of in cuts:
        steps = jax.random.uniform(jax.random.fold_in(jax.random.fold_in(key, 6), dim), (shards_of,), jnp.float32, low / len(cuts), top_value / len(cuts))
        gain = gain * jnp.repeat(jnp.exp(steps), dims[dim] // shards_of).reshape((-1,) + (1,) * (len(dims) - 1 - dim))
    return gain


def bell_draw(stream_key, dims, deviation, reach, cuts=(), held_as=jnp.bfloat16):
    values = jax.random.normal(stream_key, dims, jnp.float32) * deviation
    if len(cuts) > 0:
        values = shard_levels(stream_key, dims, cuts, -0.22, 0.18) * values
    return jnp.clip(values, min=-reach, max=reach).astype(held_as)


def setup_inputs(seed: int = 0) -> dict:
    key_of = jax.random.split(jax.random.key(seed), 7)
    anchor = bell_draw(key_of[0], (HW, D), 1.0, 6.0, ((0, 32), (1, 16)), jnp.float32)
    prev_delta = draw_prev_delta(jax.random.fold_in(key_of[6], 71), 0)
    momentum = draw_momentum(jax.random.fold_in(key_of[6], 71), 0)
    pool = bell_draw(key_of[3], (ISLANDS, ROWS, D), 1.0, 6.0, ((0, 16), (1, 32)))
    ids = with_ends(jax.random.randint(key_of[4], (ISLANDS, STEPS, TOK_ISL), 0, POOL_DEV), jax.random.fold_in(key_of[4], 1), 0, POOL_DEV - 1).astype(jnp.int32)
    cotangent = bell_draw(key_of[5], (ISLANDS, STEPS, HW, TOK_ISL), 1.0, 6.0, ((0, 16), (2, 32)))
    return {"anchor": anchor, "prev_delta": prev_delta, "momentum": momentum, "pool": pool, "ids": ids, "cotangent": cotangent}


INNER_RATE = 2.0
INNER_DECAY = 0.1
PENALTY = 0.5
MOMENT_DECAY = 0.9
OUTER_RATE = 0.7
CLIP_SHARE = 0.05

def silu_slope(preact):
    sigmoid_val = jax.nn.sigmoid(preact)
    return sigmoid_val * (1.0 + preact * (1.0 - sigmoid_val))

def reference(anchor, prev_delta, momentum, pool, ids, cotangent):
    root_width = math.sqrt(D)
    base_rows = jnp.arange(TOK_DEV * N_FSDP, dtype=jnp.int32) // TOK_DEV * POOL_DEV
    deltas = []
    for island in range(N_REPLICA):
        weights = anchor
        for inner_step in range(STEPS):
            batch = pool[island][base_rows + ids[island, inner_step]]
            rounded = weights.astype(jnp.bfloat16)
            preact = jnp.dot(rounded, batch.T, preferred_element_type=jnp.float32) / root_width
            scaled = (cotangent[island, inner_step].astype(jnp.float32) * silu_slope(preact)).astype(jnp.bfloat16)
            gradient = jnp.dot(scaled, batch, preferred_element_type=jnp.float32) / root_width
            weights = weights - INNER_RATE * gradient - INNER_DECAY * weights
        deltas.append((anchor - weights).astype(jnp.bfloat16))
    new_delta = jnp.stack(deltas)
    averaged = lax.optimization_barrier(jnp.sum(prev_delta.astype(jnp.float32), axis=0)) / N_REPLICA
    corrected = averaged + PENALTY * (averaged - momentum)
    squares = jnp.sum(corrected * corrected)
    max_norm = CLIP_SHARE * math.sqrt(D * HW)
    factor = jnp.minimum(1.0, max_norm / jnp.sqrt(squares + 1e-06))
    clipped = factor * corrected
    new_momentum = MOMENT_DECAY * momentum + clipped
    new_anchor = anchor - OUTER_RATE * (MOMENT_DECAY * new_momentum + clipped)
    return (new_delta, new_anchor, new_momentum)
```

```python
import functools
import math

import jax
import jax.numpy as jnp
from jax import lax
from jax.experimental import pallas as pl
from jax.experimental.pallas import tpu as pltpu
from jax.sharding import Mesh
from jax.sharding import PartitionSpec as P

D = 3328
HW = 3328
TOK = 1024
ROWS = 104
BLOCK = 32
EXT = 128
CHUNK = 256
GROUP = 128
COLS = 256

INNER_RATE = 2.0
INNER_DECAY = 0.1
PENALTY = 0.5
MOMENT_DECAY = 0.9
OUTER_RATE = 0.7
CLIP_SHARE = 0.05

FSDP = ("zl", "y", "c")
REPLICA = ("x", "zh")


def silu_slope(preact):
    sigmoid_val = jax.nn.sigmoid(preact)
    return sigmoid_val * (1.0 + preact * (1.0 - sigmoid_val))


def inner_kernel(anchor_ref, cot_ref, pool_hbm, delta_ref, pool, weights, rounded, folded, sems):
    copies = []
    for zl in range(2):
        for half in range(2):
            rows = pl.ds(half * 8, 8)
            copy = pltpu.make_async_copy(
                pool_hbm.at[rows, zl], pool.at[zl, rows], sems.at[zl * 2 + half]
            )
            copy.start()
            copies.append(copy)
    root_width = math.sqrt(D)

    def picks(group, step):
        part = pool[group // 4, (group % 4) * 4 : (group % 4) * 4 + 4, :, D:]
        ids = part.reshape(GROUP, EXT)[:, step : step + 1].astype(jnp.float32).astype(jnp.int32)
        token = lax.broadcasted_iota(jnp.int32, (GROUP, GROUP), 0)
        row = lax.broadcasted_iota(jnp.int32, (GROUP, GROUP), 1)
        return jnp.where(row == (token // BLOCK) * BLOCK + ids, 1.0, 0.0).astype(jnp.bfloat16)

    for step in range(2):
        for chunk in range(TOK // CHUNK):
            if step == 0:
                copies[chunk].wait()
            left = anchor_ref[...] if step == 0 else rounded[...]
            block = pool[chunk // 2, (chunk % 2) * 8 : (chunk % 2) * 8 + 8, :, :D].reshape(CHUNK, D)
            all_rows = lax.dot_general(
                left, block, (((1,), (1,)), ((), ())), preferred_element_type=jnp.float32
            )
            for part in range(CHUNK // GROUP):
                group = chunk * (CHUNK // GROUP) + part
                picked = picks(group, step)
                tokens = slice(group * GROUP, (group + 1) * GROUP)
                values = all_rows[:, part * GROUP : (part + 1) * GROUP]
                preact = jnp.zeros((ROWS, GROUP), jnp.float32)
                for _ in range(3):
                    top = values.astype(jnp.bfloat16)
                    values = values - top.astype(jnp.float32)
                    preact = preact + lax.dot_general(
                        top, picked, (((1,), (1,)), ((), ())), preferred_element_type=jnp.float32
                    )
                preact = preact / root_width
                scaled = cot_ref[step, :, tokens].astype(jnp.float32) * silu_slope(preact)
                folded[:, tokens] = jnp.dot(
                    scaled.astype(jnp.bfloat16), picked, preferred_element_type=jnp.float32
                ).astype(jnp.bfloat16)
        for start in range(0, D, COLS):
            cols = slice(start, start + COLS)
            gradient = jnp.dot(
                folded[...],
                pool[:, :, :, cols].reshape(TOK, COLS),
                preferred_element_type=jnp.float32,
            )
            before = anchor_ref[:, cols].astype(jnp.float32)
            if step == 0:
                after = before - INNER_RATE * (gradient / root_width) - INNER_DECAY * before
                weights[:, cols] = after
                rounded[:, cols] = after.astype(jnp.bfloat16)
            else:
                last = weights[:, cols]
                after = last - INNER_RATE * (gradient / root_width) - INNER_DECAY * last
                delta_ref[:, cols] = (before - after).astype(jnp.bfloat16)


def inner_steps(anchor_island, cot, gathered):
    return pl.pallas_call(
        inner_kernel,
        out_shape=jax.ShapeDtypeStruct((ROWS, D), jnp.bfloat16),
        in_specs=[
            pl.BlockSpec(memory_space=pltpu.VMEM),
            pl.BlockSpec(memory_space=pltpu.VMEM),
            pl.BlockSpec(memory_space=pl.ANY),
        ],
        out_specs=pl.BlockSpec(memory_space=pltpu.VMEM),
        scratch_shapes=[
            pltpu.VMEM((2, 16, BLOCK, D + EXT), jnp.bfloat16),
            pltpu.VMEM((ROWS, D), jnp.float32),
            pltpu.VMEM((ROWS, D), jnp.bfloat16),
            pltpu.VMEM((ROWS, TOK), jnp.bfloat16),
            pltpu.SemaphoreType.DMA((4,)),
        ],
        compiler_params=pltpu.CompilerParams(vmem_limit_bytes=32 * 1024 * 1024),
        cost_estimate=pl.CostEstimate(
            flops=4 * 2 * ROWS * TOK * D, bytes_accessed=9_000_000, transcendentals=2 * ROWS * TOK
        ),
    )(anchor_island, cot, gathered)


def swap(value, axis, mask):
    count = lax.axis_size(axis)
    return lax.ppermute(value, axis, [(i, i ^ mask) for i in range(count)])


def doubled(value, axis, mask):
    other = swap(value, axis, mask)
    second = (lax.axis_index(axis) & mask) != 0
    return jnp.concatenate(
        [jnp.where(second, other, value), jnp.where(second, value, other)], axis=0
    )


def body(anchor, prev_delta, momentum, pool, ids, cotangent):
    sampled = jnp.pad(ids[0].T.astype(jnp.bfloat16), ((0, 0), (0, EXT - ids.shape[1])))
    rows = jnp.concatenate([pool[0], sampled], axis=1)[None]
    rows = doubled(rows, "zl", 1)
    gathered = lax.all_gather(rows, ("y", "c"), axis=0)

    sums = prev_delta[0].reshape(ROWS, 16, D // 16).transpose(1, 0, 2)
    sums = lax.all_to_all(sums, REPLICA, 0, 0)
    averaged = jnp.sum(sums.astype(jnp.float32), axis=0) / 16
    corrected = averaged + PENALTY * (averaged - momentum)
    squares = jnp.sum(corrected * corrected)
    for axes, count in ((FSDP, 32), (REPLICA, 16)):
        spread = jnp.broadcast_to(squares, (count, 8, 128))
        squares = jnp.sum(lax.all_to_all(spread, axes, 0, 0)[:, 0, 0])
    max_norm = CLIP_SHARE * math.sqrt(D * HW)
    factor = jnp.minimum(1.0, max_norm / jnp.sqrt(squares + 1e-06))
    clipped = factor * corrected
    new_momentum = MOMENT_DECAY * momentum + clipped
    new_anchor = anchor - OUTER_RATE * (MOMENT_DECAY * new_momentum + clipped)

    blocks = anchor.astype(jnp.bfloat16)[None]
    for axis, mask in (("zh", 1), ("zh", 2), ("x", 1), ("x", 2)):
        blocks = doubled(blocks, axis, mask)
    anchor_island = blocks.transpose(1, 0, 2).reshape(ROWS, D)
    new_delta = inner_steps(anchor_island, cotangent[0], gathered)[None]
    return (new_delta, new_anchor, new_momentum)


def solution(mesh):
    fine = Mesh(mesh.devices.reshape(4, 4, 2, 8, 2), REPLICA + FSDP)
    return jax.shard_map(
        body,
        mesh=fine,
        in_specs=(
            P(FSDP, REPLICA),
            P(REPLICA, FSDP, None),
            P(FSDP, REPLICA),
            P(REPLICA, FSDP, None),
            P(REPLICA, None, FSDP),
            P(REPLICA, None, FSDP, None),
        ),
        out_specs=(P(REPLICA, FSDP, None), P(FSDP, REPLICA), P(FSDP, REPLICA)),
        check_vma=False,
    )
```

```python
import math

import jax
import jax.numpy as jnp
from jax import lax
from jax.experimental import pallas as pl
from jax.experimental.pallas import tpu as pltpu
from jax.sharding import Mesh
from jax.sharding import PartitionSpec as P

D = 3328
HW = 3328
TOK = 1024
ROWS = 104
BLOCK = 32
EXT = 128
CHUNK = 256
GROUP = 128
COLS = 256

INNER_RATE = 2.0
INNER_DECAY = 0.1
PENALTY = 0.5
MOMENT_DECAY = 0.9
OUTER_RATE = 0.7
CLIP_SHARE = 0.05

FSDP = ("zl", "y", "c")
REPLICA = ("x", "zh")


def silu_slope(preact):
    sigmoid_val = jax.nn.sigmoid(preact)
    return sigmoid_val * (1.0 + preact * (1.0 - sigmoid_val))


def inner_kernel(
    place_ref, anchor_ref, cot_ref, pool_hbm, delta_ref, pool, weights, rounded, folded, sems
):
    copies = []
    for zl in range(2):
        for half in range(2):
            rows = pl.ds(half * 8, 8)
            copy = pltpu.make_async_copy(
                pool_hbm.at[rows, zl ^ place_ref[0]], pool.at[zl, rows], sems.at[zl * 2 + half]
            )
            copy.start()
            copies.append(copy)
    root_width = math.sqrt(D)

    def picks(group, step):
        part = pool[group // 4, (group % 4) * 4 : (group % 4) * 4 + 4, :, D:]
        ids = part.reshape(GROUP, EXT)[:, step : step + 1].astype(jnp.float32).astype(jnp.int32)
        token = lax.broadcasted_iota(jnp.int32, (GROUP, GROUP), 0)
        row = lax.broadcasted_iota(jnp.int32, (GROUP, GROUP), 1)
        return jnp.where(row == (token // BLOCK) * BLOCK + ids, 1.0, 0.0).astype(jnp.bfloat16)

    for step in range(2):
        for chunk in range(TOK // CHUNK):
            if step == 0:
                copies[chunk].wait()
            left = anchor_ref[...] if step == 0 else rounded[...]
            block = pool[chunk // 2, (chunk % 2) * 8 : (chunk % 2) * 8 + 8, :, :D].reshape(CHUNK, D)
            all_rows = lax.dot_general(
                left, block, (((1,), (1,)), ((), ())), preferred_element_type=jnp.float32
            )
            for part in range(CHUNK // GROUP):
                group = chunk * (CHUNK // GROUP) + part
                picked = picks(group, step)
                tokens = slice(group * GROUP, (group + 1) * GROUP)
                values = all_rows[:, part * GROUP : (part + 1) * GROUP]
                preact = jnp.zeros((ROWS, GROUP), jnp.float32)
                for _ in range(3):
                    top = values.astype(jnp.bfloat16)
                    values = values - top.astype(jnp.float32)
                    preact = preact + lax.dot_general(
                        top, picked, (((1,), (1,)), ((), ())), preferred_element_type=jnp.float32
                    )
                preact = preact / root_width
                scaled = cot_ref[step, :, tokens].astype(jnp.float32) * silu_slope(preact)
                folded[:, tokens] = jnp.dot(
                    scaled.astype(jnp.bfloat16), picked, preferred_element_type=jnp.float32
                ).astype(jnp.bfloat16)
        for start in range(0, D, COLS):
            cols = slice(start, start + COLS)
            gradient = jnp.dot(
                folded[...],
                pool[:, :, :, cols].reshape(TOK, COLS),
                preferred_element_type=jnp.float32,
            )
            before = anchor_ref[:, cols].astype(jnp.float32)
            if step == 0:
                after = before - INNER_RATE * (gradient / root_width) - INNER_DECAY * before
                weights[:, cols] = after
                rounded[:, cols] = after.astype(jnp.bfloat16)
            else:
                last = weights[:, cols]
                after = last - INNER_RATE * (gradient / root_width) - INNER_DECAY * last
                delta_ref[:, cols] = (before - after).astype(jnp.bfloat16)


def inner_steps(place, anchor_island, cot, gathered):
    vmem = pl.BlockSpec(memory_space=pltpu.VMEM)
    return pl.pallas_call(
        inner_kernel,
        out_shape=jax.ShapeDtypeStruct((ROWS, D), jnp.bfloat16),
        in_specs=[
            pl.BlockSpec(memory_space=pltpu.SMEM),
            vmem,
            vmem,
            pl.BlockSpec(memory_space=pl.ANY),
        ],
        out_specs=vmem,
        scratch_shapes=[
            pltpu.VMEM((2, 16, BLOCK, D + EXT), jnp.bfloat16),
            pltpu.VMEM((ROWS, D), jnp.float32),
            pltpu.VMEM((ROWS, D), jnp.bfloat16),
            pltpu.VMEM((ROWS, TOK), jnp.bfloat16),
            pltpu.SemaphoreType.DMA((4,)),
        ],
        compiler_params=pltpu.CompilerParams(vmem_limit_bytes=50 * 1024 * 1024),
        cost_estimate=pl.CostEstimate(
            flops=4 * 2 * ROWS * TOK * D, bytes_accessed=9_000_000, transcendentals=2 * ROWS * TOK
        ),
    )(place, anchor_island, cot, gathered)


def swap(value, axis, mask):
    count = lax.axis_size(axis)
    return lax.ppermute(value, axis, [(i, i ^ mask) for i in range(count)])


def in_parts(value, shape):
    lane = lax.broadcasted_iota(jnp.int32, shape, 1)
    value = jnp.broadcast_to(value, shape)
    top = value.astype(jnp.bfloat16)
    rest = value - top.astype(jnp.float32)
    middle = rest.astype(jnp.bfloat16)
    last = (rest - middle.astype(jnp.float32)).astype(jnp.bfloat16)
    return jnp.where(lane == 0, top, jnp.where(lane == 1, middle, last))


def body(anchor, prev_delta, momentum, pool, ids, cotangent):
    tie = lax.optimization_barrier
    place = lax.axis_index("zl").reshape(1).astype(jnp.int32)
    sampled = jnp.pad(ids[0].T.astype(jnp.bfloat16), ((0, 0), (0, EXT - ids.shape[1])))
    rows = jnp.concatenate([pool[0], sampled], axis=1)
    other_rows = swap(rows, "zl", 1)
    sums = jnp.stack([prev_delta[0, :, i * (D // 4) : (i + 1) * (D // 4)] for i in range(4)])
    sums = lax.all_to_all(sums, "x", 0, 0)
    other_rows, sums = tie((other_rows, sums))
    gathered = lax.all_gather(jnp.stack([rows, other_rows]), ("y", "c"), axis=0)

    sums = jnp.sum(sums.astype(jnp.float32), axis=0)
    width = D // 16
    sums = jnp.stack([sums[:, i * width : (i + 1) * width] for i in range(4)])
    blocks = jnp.broadcast_to(anchor.astype(jnp.bfloat16), (4, ROWS, width))
    mixed = lax.all_to_all(
        jnp.concatenate([sums.astype(jnp.bfloat16), blocks], axis=1), "zh", 0, 0
    )
    averaged = jnp.sum(mixed[:, :ROWS].astype(jnp.float32), axis=0) / 16
    corrected = averaged + PENALTY * (averaged - momentum)
    note = in_parts(jnp.sum(corrected * corrected, keepdims=True), (16, width))
    blocks = jnp.concatenate([mixed[:, ROWS:].reshape(4 * ROWS, width), note], axis=0)
    blocks = lax.all_to_all(jnp.broadcast_to(blocks, (4, *blocks.shape)), "x", 0, 0)
    squares = jnp.sum(blocks[:, 4 * ROWS, :3].astype(jnp.float32))
    anchor_island = (
        blocks[:, : 4 * ROWS].reshape(16, ROWS, width).transpose(1, 0, 2).reshape(ROWS, D)
    )
    squares, anchor_island = tie((squares, anchor_island))
    spread = lax.all_to_all(jnp.broadcast_to(squares, (128, 1, 128)), ("zh", *FSDP), 0, 0)
    new_delta = inner_steps(place, anchor_island, cotangent[0], gathered)
    spread, new_delta = tie((spread, new_delta))
    squares = jnp.sum(spread[:, 0, 0])
    max_norm = CLIP_SHARE * math.sqrt(D * HW)
    factor = jnp.minimum(1.0, max_norm / jnp.sqrt(squares + 1e-06))
    clipped = factor * corrected
    new_momentum = MOMENT_DECAY * momentum + clipped
    new_anchor = anchor - OUTER_RATE * (MOMENT_DECAY * new_momentum + clipped)
    return (new_delta[None], new_anchor, new_momentum)


def solution(mesh):
    fine = Mesh(mesh.devices.reshape(4, 4, 2, 8, 2), REPLICA + FSDP)
    return jax.shard_map(
        body,
        mesh=fine,
        in_specs=(
            P(FSDP, REPLICA),
            P(REPLICA, FSDP, None),
            P(FSDP, REPLICA),
            P(REPLICA, FSDP, None),
            P(REPLICA, None, FSDP),
            P(REPLICA, None, FSDP, None),
        ),
        out_specs=(P(REPLICA, FSDP, None), P(FSDP, REPLICA), P(FSDP, REPLICA)),
        check_vma=False,
    )
```

```python
import math

import jax
import jax.numpy as jnp
from jax import lax
from jax.experimental import pallas as pl
from jax.experimental.pallas import tpu as pltpu
from jax.sharding import Mesh
from jax.sharding import PartitionSpec as P

D = 3328
HW = 3328
TOK = 1024
ROWS = 104
BLOCK = 32
EXT = 128
CHUNK = 256
COLS = 256
WIDTH = D // 16

INNER_RATE = 2.0
INNER_DECAY = 0.1
PENALTY = 0.5
MOMENT_DECAY = 0.9
OUTER_RATE = 0.7
CLIP_SHARE = 0.05

FSDP = ("zl", "y", "c")
REPLICA = ("x", "zh")


def silu_slope(preact):
    sigmoid_val = jax.nn.sigmoid(preact)
    return sigmoid_val * (1.0 + preact * (1.0 - sigmoid_val))


def inner_kernel(
    place_ref, anchor_ref, cot_ref, pool_hbm, delta_ref, pool, weights, rounded, folded, sems
):
    copies = []
    for zl in range(2):
        for half in range(2):
            rows = pl.ds(half * 8, 8)
            copy = pltpu.make_async_copy(
                pool_hbm.at[rows, zl ^ place_ref[0]], pool.at[zl, rows], sems.at[zl * 2 + half]
            )
            copy.start()
            copies.append(copy)
    root_width = math.sqrt(D)

    def picks(chunk, step):
        part = pool[chunk // 2, (chunk % 2) * 8 : (chunk % 2) * 8 + 8, :, D:]
        ids = part.reshape(CHUNK, EXT)[:, step : step + 1].astype(jnp.float32).astype(jnp.int32)
        token = lax.broadcasted_iota(jnp.int32, (CHUNK, CHUNK), 0)
        row = lax.broadcasted_iota(jnp.int32, (CHUNK, CHUNK), 1)
        return jnp.where(row == (token // BLOCK) * BLOCK + ids, 1.0, 0.0).astype(jnp.bfloat16)

    def project(chunk, step):
        if step == 0:
            copies[chunk].wait()
        left = anchor_ref[...] if step == 0 else rounded[...]
        block = pool[chunk // 2, (chunk % 2) * 8 : (chunk % 2) * 8 + 8, :, :D].reshape(CHUNK, D)
        return lax.dot_general(
            left, block, (((1,), (1,)), ((), ())), preferred_element_type=jnp.float32
        )

    def fold(chunk, step, values):
        picked = picks(chunk, step)
        tokens = slice(chunk * CHUNK, (chunk + 1) * CHUNK)
        preact = jnp.zeros((ROWS, CHUNK), jnp.float32)
        for _ in range(3):
            top = values.astype(jnp.bfloat16)
            values = values - top.astype(jnp.float32)
            preact = preact + lax.dot_general(
                top, picked, (((1,), (1,)), ((), ())), preferred_element_type=jnp.float32
            )
        preact = preact / root_width
        scaled = cot_ref[step, :, tokens].astype(jnp.float32) * silu_slope(preact)
        folded[:, tokens] = jnp.dot(
            scaled.astype(jnp.bfloat16), picked, preferred_element_type=jnp.float32
        ).astype(jnp.bfloat16)

    for step in range(2):
        values = project(0, step)
        for chunk in range(1, TOK // CHUNK):
            later = project(chunk, step)
            fold(chunk - 1, step, values)
            values = later
        fold(TOK // CHUNK - 1, step, values)
        for start in range(0, D, COLS):
            cols = slice(start, start + COLS)
            gradient = jnp.dot(
                folded[...],
                pool[:, :, :, cols].reshape(TOK, COLS),
                preferred_element_type=jnp.float32,
            )
            before = anchor_ref[:, cols].astype(jnp.float32)
            if step == 0:
                after = before - INNER_RATE * (gradient / root_width) - INNER_DECAY * before
                weights[:, cols] = after
                rounded[:, cols] = after.astype(jnp.bfloat16)
            else:
                last = weights[:, cols]
                after = last - INNER_RATE * (gradient / root_width) - INNER_DECAY * last
                delta_ref[:, cols] = (before - after).astype(jnp.bfloat16)


def inner_steps(place, anchor_island, cot, gathered):
    vmem = pl.BlockSpec(memory_space=pltpu.VMEM)
    return pl.pallas_call(
        inner_kernel,
        out_shape=jax.ShapeDtypeStruct((ROWS, D), jnp.bfloat16),
        in_specs=[
            pl.BlockSpec(memory_space=pltpu.SMEM),
            vmem,
            vmem,
            pl.BlockSpec(memory_space=pl.ANY),
        ],
        out_specs=vmem,
        scratch_shapes=[
            pltpu.VMEM((2, 16, BLOCK, D + EXT), jnp.bfloat16),
            pltpu.VMEM((ROWS, D), jnp.float32),
            pltpu.VMEM((ROWS, D), jnp.bfloat16),
            pltpu.VMEM((ROWS, TOK), jnp.bfloat16),
            pltpu.SemaphoreType.DMA((4,)),
        ],
        compiler_params=pltpu.CompilerParams(vmem_limit_bytes=50 * 1024 * 1024),
        cost_estimate=pl.CostEstimate(
            flops=4 * 2 * ROWS * TOK * D, bytes_accessed=9_000_000, transcendentals=2 * ROWS * TOK
        ),
    )(place, anchor_island, cot, gathered)


def swap(value, axis, mask):
    count = lax.axis_size(axis)
    return lax.ppermute(value, axis, [(i, i ^ mask) for i in range(count)])


def small_call(kernel, out_shapes, *args, limit=8):
    vmem = pl.BlockSpec(memory_space=pltpu.VMEM)
    return pl.pallas_call(
        kernel,
        out_shape=[jax.ShapeDtypeStruct(shape, dtype) for shape, dtype in out_shapes],
        in_specs=[vmem] * len(args),
        out_specs=[vmem] * len(out_shapes),
        compiler_params=pltpu.CompilerParams(vmem_limit_bytes=limit * 1024 * 1024),
    )(*args)


def pack_kernel(
    delta_ref, pool_ref, ids_ref, anchor_ref, momentum_ref, sums_ref, rows_ref, rounded_ref, held_ref
):
    rounded_ref[...] = anchor_ref[...].astype(jnp.bfloat16)
    held_ref[...] = momentum_ref[...]
    part = D // 4
    for i in range(4):
        sums_ref[i] = delta_ref[0, :, i * part : (i + 1) * part]
    rows_ref[:, :D] = pool_ref[0]
    ids = ids_ref[0].astype(jnp.float32)
    square = (BLOCK, BLOCK)
    diagonal = lax.broadcasted_iota(jnp.int32, square, 0) == lax.broadcasted_iota(jnp.int32, square, 1)
    lane = lax.broadcasted_iota(jnp.int32, (BLOCK, EXT), 1)
    extra = jnp.zeros((BLOCK, EXT), jnp.float32)
    for step in range(2):
        row = jnp.broadcast_to(ids[step : step + 1], square)
        column = jnp.sum(jnp.where(diagonal, row, 0.0), axis=1, keepdims=True)
        extra = jnp.where(lane == step, jnp.broadcast_to(column, extra.shape), extra)
    rows_ref[:, D:] = extra.astype(jnp.bfloat16)


def middle_kernel(sums_ref, anchor_ref, out_ref):
    sums = sum(sums_ref[i].astype(jnp.float32) for i in range(4))
    for i in range(4):
        out_ref[i, 0] = sums[:, i * WIDTH : (i + 1) * WIDTH].astype(jnp.bfloat16)
        out_ref[i, 1] = anchor_ref[...]


def square_kernel(mixed_ref, momentum_ref, corrected_ref, out_ref):
    averaged = sum(mixed_ref[i, 0].astype(jnp.float32) for i in range(4)) / 16
    corrected = averaged + PENALTY * (averaged - momentum_ref[...])
    corrected_ref[...] = corrected
    squares = jnp.sum(corrected * corrected, axis=(0, 1), keepdims=True)
    shape = (ROWS, 256 - WIDTH)
    lane = lax.broadcasted_iota(jnp.int32, shape, 1)
    squares = jnp.broadcast_to(squares, shape)
    top = squares.astype(jnp.bfloat16).astype(jnp.float32)
    middle = (squares - top).astype(jnp.bfloat16).astype(jnp.float32)
    note = jnp.where(lane == 0, top, jnp.where(lane == 1, middle, squares - top - middle))
    note = jnp.where(lane < 3, note, 0.0).astype(jnp.bfloat16)
    for i in range(4):
        for j in range(4):
            out_ref[i, j, :, :WIDTH] = mixed_ref[j, 1]
            out_ref[i, j, :, WIDTH:] = note


def unpack_kernel(blocks_ref, anchor_ref, spread_ref):
    shape = (ROWS, 128)
    lane = lax.broadcasted_iota(jnp.int32, shape, 1)
    row = lax.broadcasted_iota(jnp.int32, shape, 0)
    squares = jnp.zeros(shape, jnp.float32)
    for i in range(4):
        for j in range(4):
            place = (i * 4 + j) * WIDTH
            anchor_ref[:, place : place + WIDTH] = blocks_ref[i, j, :, :WIDTH]
        squares = squares + blocks_ref[i, 0, :, 128:].astype(jnp.float32)
    squares = jnp.where((row == 0) & (lane >= WIDTH - 128), squares, 0.0)
    squares = jnp.sum(squares, axis=(0, 1), keepdims=True)
    spread_ref[...] = jnp.broadcast_to(squares.reshape(1, 1, 1), spread_ref.shape)


def outer_kernel(spread_ref, corrected_ref, momentum_ref, anchor_ref, new_anchor_ref, new_momentum_ref):
    squares = jnp.sum(spread_ref[...], axis=0)[:, :1]
    max_norm = CLIP_SHARE * math.sqrt(D * HW)
    factor = jnp.minimum(1.0, max_norm / jnp.sqrt(squares + 1e-06))
    clipped = factor * corrected_ref[...]
    new_momentum = MOMENT_DECAY * momentum_ref[...] + clipped
    new_momentum_ref[...] = new_momentum
    new_anchor_ref[...] = anchor_ref[...] - OUTER_RATE * (MOMENT_DECAY * new_momentum + clipped)


def body(anchor, prev_delta, momentum, pool, ids, cotangent):
    tie = lax.optimization_barrier
    bf16, f32 = jnp.bfloat16, jnp.float32
    block = (ROWS, WIDTH)
    place = lax.axis_index("zl").reshape(1).astype(jnp.int32)
    sums, rows, rounded, held = small_call(
        pack_kernel,
        [((4, ROWS, D // 4), bf16), ((BLOCK, D + EXT), bf16), (block, bf16), (block, f32)],
        prev_delta,
        pool,
        ids,
        anchor,
        momentum,
        limit=56,
    )
    sums = lax.all_to_all(sums, "x", 0, 0)
    other_rows, sums = tie((swap(rows, "zl", 1), sums))
    gathered = lax.all_gather(jnp.stack([rows, other_rows]), ("y", "c"), axis=0)

    (mixed,) = small_call(middle_kernel, [((4, 2, *block), bf16)], sums, rounded)
    mixed = lax.all_to_all(mixed, "zh", 0, 0)
    corrected, blocks = small_call(
        square_kernel, [(block, f32), ((4, 4, ROWS, 256), bf16)], mixed, held
    )
    blocks = lax.all_to_all(blocks, "x", 0, 0)
    anchor_island, spread = small_call(
        unpack_kernel, [((ROWS, D), bf16), ((128, 1, 128), f32)], blocks
    )
    spread = lax.all_to_all(spread, ("zh", *FSDP), 0, 0)
    new_delta = inner_steps(place, anchor_island, cotangent[0], gathered)
    spread, new_delta = tie((spread, new_delta))
    new_anchor, new_momentum = small_call(
        outer_kernel, [(block, f32), (block, f32)], spread, corrected, momentum, anchor
    )
    return (new_delta[None], new_anchor, new_momentum)


def solution(mesh):
    fine = Mesh(mesh.devices.reshape(4, 4, 2, 8, 2), REPLICA + FSDP)
    return jax.shard_map(
        body,
        mesh=fine,
        in_specs=(
            P(FSDP, REPLICA),
            P(REPLICA, FSDP, None),
            P(FSDP, REPLICA),
            P(REPLICA, FSDP, None),
            P(REPLICA, None, FSDP),
            P(REPLICA, None, FSDP, None),
        ),
        out_specs=(P(REPLICA, FSDP, None), P(FSDP, REPLICA), P(FSDP, REPLICA)),
        check_vma=False,
    )
```

```python
import math

import jax
import jax.numpy as jnp
from jax import lax
from jax.experimental import pallas as pl
from jax.experimental.pallas import tpu as pltpu
from jax.sharding import Mesh
from jax.sharding import PartitionSpec as P

D = 3328
HW = 3328
TOK = 1024
ROWS = 104
BLOCK = 32
EXT = 128
CHUNK = 256
COLS = 256
WIDTH = D // 16
WINDOW = 896

INNER_RATE = 2.0
INNER_DECAY = 0.1
PENALTY = 0.5
MOMENT_DECAY = 0.9
OUTER_RATE = 0.7
CLIP_SHARE = 0.05

FSDP = ("zl", "y", "c")
REPLICA = ("x", "zh")


def silu_slope(preact):
    sigmoid_val = jax.nn.sigmoid(preact)
    return sigmoid_val * (1.0 + preact * (1.0 - sigmoid_val))


def inner_kernel(
    place_ref, anchor_ref, cot_ref, pool_hbm, delta_ref, pool, weights, rounded, folded, sems
):
    copies = []
    for zl in range(2):
        for half in range(2):
            rows = pl.ds(half * 8, 8)
            copy = pltpu.make_async_copy(
                pool_hbm.at[rows, zl ^ place_ref[0]], pool.at[zl, rows], sems.at[zl * 2 + half]
            )
            copy.start()
            copies.append(copy)
    root_width = math.sqrt(D)

    def picks(chunk, step):
        part = pool[chunk // 2, (chunk % 2) * 8 : (chunk % 2) * 8 + 8, :, D:]
        ids = part.reshape(CHUNK, EXT)[:, step : step + 1].astype(jnp.float32).astype(jnp.int32)
        token = lax.broadcasted_iota(jnp.int32, (CHUNK, CHUNK), 0)
        row = lax.broadcasted_iota(jnp.int32, (CHUNK, CHUNK), 1)
        return jnp.where(row == (token // BLOCK) * BLOCK + ids, 1.0, 0.0).astype(jnp.bfloat16)

    def project(chunk, step):
        if step == 0:
            copies[chunk].wait()
        left = anchor_ref[...] if step == 0 else rounded[...]
        block = pool[chunk // 2, (chunk % 2) * 8 : (chunk % 2) * 8 + 8, :, :D].reshape(CHUNK, D)
        return lax.dot_general(
            left, block, (((1,), (1,)), ((), ())), preferred_element_type=jnp.float32
        )

    def fold(chunk, step, values):
        picked = picks(chunk, step)
        tokens = slice(chunk * CHUNK, (chunk + 1) * CHUNK)
        preact = jnp.zeros((ROWS, CHUNK), jnp.float32)
        for _ in range(3):
            top = values.astype(jnp.bfloat16)
            values = values - top.astype(jnp.float32)
            preact = preact + lax.dot_general(
                top, picked, (((1,), (1,)), ((), ())), preferred_element_type=jnp.float32
            )
        preact = preact / root_width
        scaled = cot_ref[step, :, tokens].astype(jnp.float32) * silu_slope(preact)
        folded[:, tokens] = jnp.dot(
            scaled.astype(jnp.bfloat16), picked, preferred_element_type=jnp.float32
        ).astype(jnp.bfloat16)

    for step in range(2):
        values = project(0, step)
        for chunk in range(1, TOK // CHUNK):
            later = project(chunk, step)
            fold(chunk - 1, step, values)
            values = later
        fold(TOK // CHUNK - 1, step, values)
        for start in range(0, D, COLS):
            cols = slice(start, start + COLS)
            gradient = jnp.dot(
                folded[...],
                pool[:, :, :, cols].reshape(TOK, COLS),
                preferred_element_type=jnp.float32,
            )
            before = anchor_ref[:, cols].astype(jnp.float32)
            if step == 0:
                after = before - INNER_RATE * (gradient / root_width) - INNER_DECAY * before
                weights[:, cols] = after
                rounded[:, cols] = after.astype(jnp.bfloat16)
            else:
                last = weights[:, cols]
                after = last - INNER_RATE * (gradient / root_width) - INNER_DECAY * last
                delta_ref[:, cols] = (before - after).astype(jnp.bfloat16)


def inner_steps(place, anchor_island, cot, gathered):
    vmem = pl.BlockSpec(memory_space=pltpu.VMEM)
    return pl.pallas_call(
        inner_kernel,
        out_shape=jax.ShapeDtypeStruct((ROWS, D), jnp.bfloat16),
        in_specs=[
            pl.BlockSpec(memory_space=pltpu.SMEM),
            vmem,
            vmem,
            pl.BlockSpec(memory_space=pl.ANY),
        ],
        out_specs=vmem,
        scratch_shapes=[
            pltpu.VMEM((2, 16, BLOCK, D + EXT), jnp.bfloat16),
            pltpu.VMEM((ROWS, D), jnp.float32),
            pltpu.VMEM((ROWS, D), jnp.bfloat16),
            pltpu.VMEM((ROWS, TOK), jnp.bfloat16),
            pltpu.SemaphoreType.DMA((4,)),
        ],
        compiler_params=pltpu.CompilerParams(vmem_limit_bytes=50 * 1024 * 1024),
        cost_estimate=pl.CostEstimate(
            flops=4 * 2 * ROWS * TOK * D, bytes_accessed=9_000_000, transcendentals=2 * ROWS * TOK
        ),
    )(place, anchor_island, cot, gathered)


def swap(value, axis, mask):
    count = lax.axis_size(axis)
    return lax.ppermute(value, axis, [(i, i ^ mask) for i in range(count)])


def small_call(kernel, out_shapes, *args):
    vmem = pl.BlockSpec(memory_space=pltpu.VMEM)
    return pl.pallas_call(
        kernel,
        out_shape=[jax.ShapeDtypeStruct(shape, dtype) for shape, dtype in out_shapes],
        in_specs=[vmem] * len(args),
        out_specs=[vmem] * len(out_shapes),
        compiler_params=pltpu.CompilerParams(vmem_limit_bytes=8 * 1024 * 1024),
    )(*args)


def window_kernel(delta_hbm, sums_ref, sems):
    copies = [
        pltpu.make_async_copy(
            delta_hbm.at[0, :, pl.ds(i * (D // 4) // 128 * 128, WINDOW)], sums_ref.at[i], sems.at[i]
        )
        for i in range(4)
    ]
    for copy in copies:
        copy.start()
    for copy in copies:
        copy.wait()


def windows(prev_delta):
    return pl.pallas_call(
        window_kernel,
        out_shape=jax.ShapeDtypeStruct((4, ROWS, WINDOW), jnp.bfloat16),
        in_specs=[pl.BlockSpec(memory_space=pl.ANY)],
        out_specs=pl.BlockSpec(memory_space=pltpu.VMEM),
        scratch_shapes=[pltpu.SemaphoreType.DMA((4,))],
        compiler_params=pltpu.CompilerParams(vmem_limit_bytes=56 * 1024 * 1024),
    )(prev_delta)


def middle_kernel(place_ref, sums_ref, anchor_ref, out_ref):
    sums = sum(sums_ref[i].astype(jnp.float32) for i in range(4))
    sums = jnp.where(place_ref[1] % 2 == 1, sums[:, WINDOW - D // 4 :], sums[:, : D // 4])
    for i in range(4):
        out_ref[i, 0] = sums[:, i * WIDTH : (i + 1) * WIDTH].astype(jnp.bfloat16)
        out_ref[i, 1] = anchor_ref[...]


def square_kernel(mixed_ref, stale_ref, corrected_ref, out_ref):
    averaged = sum(mixed_ref[i, 0].astype(jnp.float32) for i in range(4)) / 16
    corrected = averaged + (PENALTY * averaged - stale_ref[...])
    corrected_ref[...] = corrected
    squares = jnp.sum(corrected * corrected, axis=(0, 1), keepdims=True)
    shape = (ROWS, WINDOW - D // 4)
    lane = lax.broadcasted_iota(jnp.int32, shape, 1)
    squares = jnp.broadcast_to(squares, shape)
    top = squares.astype(jnp.bfloat16).astype(jnp.float32)
    middle = (squares - top).astype(jnp.bfloat16).astype(jnp.float32)
    note = jnp.where(lane == 0, top, jnp.where(lane == 1, middle, squares - top - middle))
    note = jnp.where(lane < 3, note, 0.0).astype(jnp.bfloat16)
    for j in range(4):
        block = mixed_ref[j, 1]
        for i in range(4):
            out_ref[i, :, j * WIDTH : (j + 1) * WIDTH] = block
    for i in range(4):
        out_ref[i, :, D // 4 :] = note


def unpack_kernel(blocks_ref, anchor_ref, spread_ref):
    shape = (ROWS, 128)
    lane = lax.broadcasted_iota(jnp.int32, shape, 1)
    row = lax.broadcasted_iota(jnp.int32, shape, 0)
    squares = jnp.zeros(shape, jnp.float32)
    for i in range(4):
        anchor_ref[:, i * (D // 4) : (i + 1) * (D // 4)] = blocks_ref[i, :, : D // 4]
        squares = squares + blocks_ref[i, :, WINDOW - 128 :].astype(jnp.float32)
    squares = jnp.where((row == 0) & (lane >= 128 - (WINDOW - D // 4)), squares, 0.0)
    squares = jnp.sum(squares, axis=(0, 1), keepdims=True)
    spread_ref[...] = jnp.broadcast_to(squares.reshape(1, 1, 1), spread_ref.shape)


def outer_kernel(spread_ref, corrected_ref, momentum_ref, anchor_ref, new_anchor_ref, new_momentum_ref):
    squares = jnp.sum(spread_ref[...], axis=0)[:, :1]
    max_norm = CLIP_SHARE * math.sqrt(D * HW)
    factor = jnp.minimum(1.0, max_norm / jnp.sqrt(squares + 1e-06))
    clipped = factor * corrected_ref[...]
    new_momentum = MOMENT_DECAY * momentum_ref[...] + clipped
    new_momentum_ref[...] = new_momentum
    new_anchor_ref[...] = anchor_ref[...] - OUTER_RATE * (MOMENT_DECAY * new_momentum + clipped)


def middle(place, sums, rounded):
    vmem = pl.BlockSpec(memory_space=pltpu.VMEM)
    return pl.pallas_call(
        middle_kernel,
        out_shape=[jax.ShapeDtypeStruct((4, 2, ROWS, WIDTH), jnp.bfloat16)],
        in_specs=[pl.BlockSpec(memory_space=pltpu.SMEM), vmem, vmem],
        out_specs=[vmem],
        compiler_params=pltpu.CompilerParams(vmem_limit_bytes=8 * 1024 * 1024),
    )(place, sums, rounded)


def body(anchor, prev_delta, momentum, pool, ids, cotangent):
    tie = lax.optimization_barrier
    bf16, f32 = jnp.bfloat16, jnp.float32
    block = (ROWS, WIDTH)
    place = jnp.stack([lax.axis_index("zl"), lax.axis_index("x")]).astype(jnp.int32)
    sampled = jnp.pad(ids[0].T.astype(bf16), ((0, 0), (0, EXT - ids.shape[1])))
    rows = jnp.concatenate([pool[0], sampled], axis=1)
    other_rows = swap(rows, "zl", 1)
    sums = windows(prev_delta)
    rounded = anchor.astype(bf16)
    stale = PENALTY * momentum
    other_rows, sums, rounded, stale = tie((other_rows, sums, rounded, stale))
    gathered = lax.all_gather(jnp.stack([rows, other_rows]), ("y", "c"), axis=0)

    sums = lax.all_to_all(sums, "x", 0, 0)
    (mixed,) = middle(place, sums, rounded)
    mixed = lax.all_to_all(mixed, "zh", 0, 0)
    corrected, blocks = small_call(
        square_kernel, [(block, f32), ((4, ROWS, WINDOW), bf16)], mixed, stale
    )
    blocks = lax.all_to_all(blocks, "x", 0, 0)
    anchor_island, spread = small_call(
        unpack_kernel, [((ROWS, D), bf16), ((128, 1, 128), f32)], blocks
    )
    spread = lax.all_to_all(spread, ("zh", *FSDP), 0, 0)
    new_delta = inner_steps(place, anchor_island, cotangent[0], gathered)
    spread, new_delta = tie((spread, new_delta))
    new_anchor, new_momentum = small_call(
        outer_kernel, [(block, f32), (block, f32)], spread, corrected, momentum, anchor
    )
    return (new_delta[None], new_anchor, new_momentum)


def solution(mesh):
    fine = Mesh(mesh.devices.reshape(4, 4, 2, 8, 2), REPLICA + FSDP)
    return jax.shard_map(
        body,
        mesh=fine,
        in_specs=(
            P(FSDP, REPLICA),
            P(REPLICA, FSDP, None),
            P(FSDP, REPLICA),
            P(REPLICA, FSDP, None),
            P(REPLICA, None, FSDP),
            P(REPLICA, None, FSDP, None),
        ),
        out_specs=(P(REPLICA, FSDP, None), P(FSDP, REPLICA), P(FSDP, REPLICA)),
        check_vma=False,
    )
```

```python
import math

import jax
import jax.numpy as jnp
from jax import lax
from jax.experimental import pallas as pl
from jax.experimental.pallas import tpu as pltpu
from jax.sharding import Mesh
from jax.sharding import PartitionSpec as P

D = 3328
HW = 3328
TOK = 1024
ROWS = 104
BLOCK = 32
EXT = 128
CHUNK = 256
COLS = 256
WIDTH = D // 16
WINDOW = 896

INNER_RATE = 2.0
INNER_DECAY = 0.1
PENALTY = 0.5
MOMENT_DECAY = 0.9
OUTER_RATE = 0.7
CLIP_SHARE = 0.05

FSDP = ("zl", "y", "c")
REPLICA = ("x", "zh")


def silu_slope(preact):
    sigmoid_val = jax.nn.sigmoid(preact)
    return sigmoid_val * (1.0 + preact * (1.0 - sigmoid_val))


def inner_kernel(
    place_ref, anchor_ref, cot_ref, pool_hbm, delta_ref, pool, weights, rounded, folded, sems
):
    copies = []
    for zl in range(2):
        for half in range(2):
            rows = pl.ds(half * 8, 8)
            copy = pltpu.make_async_copy(
                pool_hbm.at[rows, zl ^ place_ref[0]], pool.at[zl, rows], sems.at[zl * 2 + half]
            )
            copy.start()
            copies.append(copy)
    root_width = math.sqrt(D)

    def picks(chunk, step):
        part = pool[chunk // 2, (chunk % 2) * 8 : (chunk % 2) * 8 + 8, :, D:]
        ids = part.reshape(CHUNK, EXT)[:, step : step + 1].astype(jnp.float32).astype(jnp.int32)
        token = lax.broadcasted_iota(jnp.int32, (CHUNK, CHUNK), 0)
        row = lax.broadcasted_iota(jnp.int32, (CHUNK, CHUNK), 1)
        return jnp.where(row == (token // BLOCK) * BLOCK + ids, 1.0, 0.0).astype(jnp.bfloat16)

    def project(chunk, step):
        if step == 0:
            copies[chunk].wait()
        left = anchor_ref[...] if step == 0 else rounded[...]
        block = pool[chunk // 2, (chunk % 2) * 8 : (chunk % 2) * 8 + 8, :, :D].reshape(CHUNK, D)
        return lax.dot_general(
            left, block, (((1,), (1,)), ((), ())), preferred_element_type=jnp.float32
        )

    def fold(chunk, step, values):
        picked = picks(chunk, step)
        tokens = slice(chunk * CHUNK, (chunk + 1) * CHUNK)
        preact = jnp.zeros((ROWS, CHUNK), jnp.float32)
        for _ in range(3):
            top = values.astype(jnp.bfloat16)
            values = values - top.astype(jnp.float32)
            preact = preact + lax.dot_general(
                top, picked, (((1,), (1,)), ((), ())), preferred_element_type=jnp.float32
            )
        preact = preact / root_width
        scaled = cot_ref[step, :, tokens].astype(jnp.float32) * silu_slope(preact)
        folded[:, tokens] = jnp.dot(
            scaled.astype(jnp.bfloat16), picked, preferred_element_type=jnp.float32
        ).astype(jnp.bfloat16)

    for step in range(2):
        values = project(0, step)
        for chunk in range(1, TOK // CHUNK):
            later = project(chunk, step)
            fold(chunk - 1, step, values)
            values = later
        fold(TOK // CHUNK - 1, step, values)
        for start in range(0, D, COLS):
            cols = slice(start, start + COLS)
            gradient = jnp.dot(
                folded[...],
                pool[:, :, :, cols].reshape(TOK, COLS),
                preferred_element_type=jnp.float32,
            )
            before = anchor_ref[:, cols].astype(jnp.float32)
            if step == 0:
                after = before - INNER_RATE * (gradient / root_width) - INNER_DECAY * before
                weights[:, cols] = after
                rounded[:, cols] = after.astype(jnp.bfloat16)
            else:
                last = weights[:, cols]
                after = last - INNER_RATE * (gradient / root_width) - INNER_DECAY * last
                delta_ref[:, cols] = (before - after).astype(jnp.bfloat16)


def inner_steps(place, anchor_island, cot, gathered):
    vmem = pl.BlockSpec(memory_space=pltpu.VMEM)
    return pl.pallas_call(
        inner_kernel,
        out_shape=jax.ShapeDtypeStruct((ROWS, D), jnp.bfloat16),
        in_specs=[
            pl.BlockSpec(memory_space=pltpu.SMEM),
            vmem,
            vmem,
            pl.BlockSpec(memory_space=pl.ANY),
        ],
        out_specs=vmem,
        scratch_shapes=[
            pltpu.VMEM((2, 16, BLOCK, D + EXT), jnp.bfloat16),
            pltpu.VMEM((ROWS, D), jnp.float32),
            pltpu.VMEM((ROWS, D), jnp.bfloat16),
            pltpu.VMEM((ROWS, TOK), jnp.bfloat16),
            pltpu.SemaphoreType.DMA((4,)),
        ],
        compiler_params=pltpu.CompilerParams(vmem_limit_bytes=50 * 1024 * 1024),
        cost_estimate=pl.CostEstimate(
            flops=4 * 2 * ROWS * TOK * D, bytes_accessed=9_000_000, transcendentals=2 * ROWS * TOK
        ),
    )(place, anchor_island, cot, gathered)


def swap(value, axis, mask):
    count = lax.axis_size(axis)
    return lax.ppermute(value, axis, [(i, i ^ mask) for i in range(count)])


def small_call(kernel, out_shapes, *args):
    vmem = pl.BlockSpec(memory_space=pltpu.VMEM)
    return pl.pallas_call(
        kernel,
        out_shape=[jax.ShapeDtypeStruct(shape, dtype) for shape, dtype in out_shapes],
        in_specs=[vmem] * len(args),
        out_specs=[vmem] * len(out_shapes),
        compiler_params=pltpu.CompilerParams(vmem_limit_bytes=8 * 1024 * 1024),
    )(*args)


def window_kernel(delta_hbm, sums_ref, sems):
    copies = [
        pltpu.make_async_copy(
            delta_hbm.at[0, :, pl.ds(i * (D // 4) // 128 * 128, WINDOW)], sums_ref.at[i], sems.at[i]
        )
        for i in range(4)
    ]
    for copy in copies:
        copy.start()
    for copy in copies:
        copy.wait()


def windows(prev_delta):
    return pl.pallas_call(
        window_kernel,
        out_shape=jax.ShapeDtypeStruct((4, ROWS, WINDOW), jnp.bfloat16),
        in_specs=[pl.BlockSpec(memory_space=pl.ANY)],
        out_specs=pl.BlockSpec(memory_space=pltpu.VMEM),
        scratch_shapes=[pltpu.SemaphoreType.DMA((4,))],
        compiler_params=pltpu.CompilerParams(vmem_limit_bytes=56 * 1024 * 1024),
    )(prev_delta)


def middle_kernel(place_ref, sums_ref, anchor_ref, out_ref):
    sums = sum(sums_ref[i].astype(jnp.float32) for i in range(4))
    sums = jnp.where(place_ref[1] % 2 == 1, sums[:, WINDOW - D // 4 :], sums[:, : D // 4])
    for i in range(4):
        out_ref[i, 0] = sums[:, i * WIDTH : (i + 1) * WIDTH].astype(jnp.bfloat16)
        out_ref[i, 1] = anchor_ref[...]


def square_kernel(mixed_ref, stale_ref, corrected_ref, out_ref):
    averaged = sum(mixed_ref[i, 0].astype(jnp.float32) for i in range(4)) / 16
    corrected = averaged + (PENALTY * averaged - stale_ref[...])
    corrected_ref[...] = corrected
    squares = jnp.sum(corrected * corrected, axis=(0, 1), keepdims=True)
    shape = (ROWS, WINDOW - D // 4)
    lane = lax.broadcasted_iota(jnp.int32, shape, 1)
    squares = jnp.broadcast_to(squares, shape)
    top = squares.astype(jnp.bfloat16).astype(jnp.float32)
    middle = (squares - top).astype(jnp.bfloat16).astype(jnp.float32)
    note = jnp.where(lane == 0, top, jnp.where(lane == 1, middle, squares - top - middle))
    note = jnp.where(lane < 3, note, 0.0).astype(jnp.bfloat16)
    for j in range(4):
        block = mixed_ref[j, 1]
        for i in range(4):
            out_ref[i, :, j * WIDTH : (j + 1) * WIDTH] = block
    for i in range(4):
        out_ref[i, :, D // 4 :] = note


def unpack_kernel(blocks_ref, anchor_ref, spread_ref):
    shape = (ROWS, 128)
    lane = lax.broadcasted_iota(jnp.int32, shape, 1)
    row = lax.broadcasted_iota(jnp.int32, shape, 0)
    squares = jnp.zeros(shape, jnp.float32)
    for i in range(4):
        anchor_ref[:, i * (D // 4) : (i + 1) * (D // 4)] = blocks_ref[i, :, : D // 4]
        squares = squares + blocks_ref[i, :, WINDOW - 128 :].astype(jnp.float32)
    squares = jnp.where((row == 0) & (lane >= 128 - (WINDOW - D // 4)), squares, 0.0)
    squares = jnp.sum(squares, axis=(0, 1), keepdims=True)
    spread_ref[...] = jnp.broadcast_to(squares.reshape(1, 1, 1), spread_ref.shape)


def outer_kernel(spread_ref, corrected_ref, momentum_ref, anchor_ref, new_anchor_ref, new_momentum_ref):
    squares = jnp.sum(spread_ref[...], axis=0)[:, :1]
    max_norm = CLIP_SHARE * math.sqrt(D * HW)
    factor = jnp.minimum(1.0, max_norm / jnp.sqrt(squares + 1e-06))
    clipped = factor * corrected_ref[...]
    new_momentum = MOMENT_DECAY * momentum_ref[...] + clipped
    new_momentum_ref[...] = new_momentum
    new_anchor_ref[...] = anchor_ref[...] - OUTER_RATE * (MOMENT_DECAY * new_momentum + clipped)


def middle(place, sums, rounded):
    vmem = pl.BlockSpec(memory_space=pltpu.VMEM)
    return pl.pallas_call(
        middle_kernel,
        out_shape=[jax.ShapeDtypeStruct((4, 2, ROWS, WIDTH), jnp.bfloat16)],
        in_specs=[pl.BlockSpec(memory_space=pltpu.SMEM), vmem, vmem],
        out_specs=[vmem],
        compiler_params=pltpu.CompilerParams(vmem_limit_bytes=8 * 1024 * 1024),
        cost_estimate=pl.CostEstimate(flops=200000000000, bytes_accessed=1_000_000, transcendentals=0),
    )(place, sums, rounded)


def body(anchor, prev_delta, momentum, pool, ids, cotangent):
    tie = lax.optimization_barrier
    bf16, f32 = jnp.bfloat16, jnp.float32
    block = (ROWS, WIDTH)
    place = jnp.stack([lax.axis_index("zl"), lax.axis_index("x")]).astype(jnp.int32)
    sampled = jnp.pad(ids[0].T, ((0, 0), (0, EXT - ids.shape[1]))).astype(bf16)
    rows = jnp.concatenate([pool[0], sampled], axis=1)
    other_rows = swap(rows, "zl", 1)
    sums = windows(prev_delta)
    pairs, held_anchor, held_momentum = tie((jnp.stack([rows, other_rows]), anchor, momentum))
    gathered = lax.all_gather(pairs, ("y", "c"), axis=0)
    rounded = held_anchor.astype(bf16)
    stale = PENALTY * held_momentum

    sums = lax.all_to_all(sums, "x", 0, 0)
    (mixed,) = middle(place, sums, rounded)
    mixed = lax.all_to_all(mixed, "zh", 0, 0)
    corrected, blocks = small_call(
        square_kernel, [(block, f32), ((4, ROWS, WINDOW), bf16)], mixed, stale
    )
    blocks = lax.all_to_all(blocks, "x", 0, 0)
    anchor_island, spread = small_call(
        unpack_kernel, [((ROWS, D), bf16), ((128, 1, 128), f32)], blocks
    )
    spread = lax.all_to_all(spread, ("zh", *FSDP), 0, 0)
    new_delta = inner_steps(place, anchor_island, cotangent[0], gathered)
    spread, new_delta = tie((spread, new_delta))
    new_anchor, new_momentum = small_call(
        outer_kernel, [(block, f32), (block, f32)], spread, corrected, momentum, anchor
    )
    return (new_delta[None], new_anchor, new_momentum)


def solution(mesh):
    fine = Mesh(mesh.devices.reshape(4, 4, 2, 8, 2), REPLICA + FSDP)
    return jax.shard_map(
        body,
        mesh=fine,
        in_specs=(
            P(FSDP, REPLICA),
            P(REPLICA, FSDP, None),
            P(FSDP, REPLICA),
            P(REPLICA, FSDP, None),
            P(REPLICA, None, FSDP),
            P(REPLICA, None, FSDP, None),
        ),
        out_specs=(P(REPLICA, FSDP, None), P(FSDP, REPLICA), P(FSDP, REPLICA)),
        check_vma=False,
    )
```

```python
import math

import jax
import jax.numpy as jnp
from jax import lax
from jax.experimental import pallas as pl
from jax.experimental.pallas import tpu as pltpu
from jax.sharding import Mesh
from jax.sharding import PartitionSpec as P

D = 3328
HW = 3328
TOK = 1024
ROWS = 104
BLOCK = 32
EXT = 128
CHUNK = 256
COLS = 256
WIDTH = D // 16
WINDOW = 896

INNER_RATE = 2.0
INNER_DECAY = 0.1
PENALTY = 0.5
MOMENT_DECAY = 0.9
OUTER_RATE = 0.7
CLIP_SHARE = 0.05

FSDP = ("zl", "y", "c")
REPLICA = ("x", "zh")


def silu_slope(preact):
    sigmoid_val = jax.nn.sigmoid(preact)
    return sigmoid_val * (1.0 + preact * (1.0 - sigmoid_val))


def inner_kernel(
    place_ref, anchor_ref, cot_ref, pool_hbm, delta_ref, pool, weights, rounded, folded, sems
):
    copies = []
    for zl in range(2):
        for half in range(2):
            rows = pl.ds(half * 8, 8)
            copy = pltpu.make_async_copy(
                pool_hbm.at[rows, zl ^ place_ref[0]], pool.at[zl, rows], sems.at[zl * 2 + half]
            )
            copy.start()
            copies.append(copy)
    root_width = math.sqrt(D)

    def picks(chunk, step):
        part = pool[chunk // 2, (chunk % 2) * 8 : (chunk % 2) * 8 + 8, :, D:]
        ids = part.reshape(CHUNK, EXT)[:, step : step + 1].astype(jnp.float32).astype(jnp.int32)
        token = lax.broadcasted_iota(jnp.int32, (CHUNK, CHUNK), 0)
        row = lax.broadcasted_iota(jnp.int32, (CHUNK, CHUNK), 1)
        return jnp.where(row == (token // BLOCK) * BLOCK + ids, 1.0, 0.0).astype(jnp.bfloat16)

    def project(chunk, step):
        if step == 0:
            copies[chunk].wait()
        left = anchor_ref[...] if step == 0 else rounded[...]
        block = pool[chunk // 2, (chunk % 2) * 8 : (chunk % 2) * 8 + 8, :, :D].reshape(CHUNK, D)
        return lax.dot_general(
            left, block, (((1,), (1,)), ((), ())), preferred_element_type=jnp.float32
        )

    def fold(chunk, step, values):
        picked = picks(chunk, step)
        tokens = slice(chunk * CHUNK, (chunk + 1) * CHUNK)
        preact = jnp.zeros((ROWS, CHUNK), jnp.float32)
        for _ in range(2):
            top = values.astype(jnp.bfloat16)
            values = values - top.astype(jnp.float32)
            preact = preact + lax.dot_general(
                top, picked, (((1,), (1,)), ((), ())), preferred_element_type=jnp.float32
            )
        preact = preact / root_width
        scaled = cot_ref[step, :, tokens].astype(jnp.float32) * silu_slope(preact)
        folded[:, tokens] = jnp.dot(
            scaled.astype(jnp.bfloat16), picked, preferred_element_type=jnp.float32
        ).astype(jnp.bfloat16)

    for step in range(2):
        values = project(0, step)
        for chunk in range(1, TOK // CHUNK):
            later = project(chunk, step)
            fold(chunk - 1, step, values)
            values = later
        fold(TOK // CHUNK - 1, step, values)
        for start in range(0, D, COLS):
            cols = slice(start, start + COLS)
            gradient = jnp.dot(
                folded[...],
                pool[:, :, :, cols].reshape(TOK, COLS),
                preferred_element_type=jnp.float32,
            )
            before = anchor_ref[:, cols].astype(jnp.float32)
            if step == 0:
                after = before - INNER_RATE * (gradient / root_width) - INNER_DECAY * before
                weights[:, cols] = after
                rounded[:, cols] = after.astype(jnp.bfloat16)
            else:
                last = weights[:, cols]
                after = last - INNER_RATE * (gradient / root_width) - INNER_DECAY * last
                delta_ref[:, cols] = (before - after).astype(jnp.bfloat16)


def inner_steps(place, anchor_island, cot, gathered):
    vmem = pl.BlockSpec(memory_space=pltpu.VMEM)
    return pl.pallas_call(
        inner_kernel,
        out_shape=jax.ShapeDtypeStruct((ROWS, D), jnp.bfloat16),
        in_specs=[
            pl.BlockSpec(memory_space=pltpu.SMEM),
            vmem,
            vmem,
            pl.BlockSpec(memory_space=pl.ANY),
        ],
        out_specs=vmem,
        scratch_shapes=[
            pltpu.VMEM((2, 16, BLOCK, D + EXT), jnp.bfloat16),
            pltpu.VMEM((ROWS, D), jnp.float32),
            pltpu.VMEM((ROWS, D), jnp.bfloat16),
            pltpu.VMEM((ROWS, TOK), jnp.bfloat16),
            pltpu.SemaphoreType.DMA((4,)),
        ],
        compiler_params=pltpu.CompilerParams(vmem_limit_bytes=50 * 1024 * 1024),
        cost_estimate=pl.CostEstimate(
            flops=4 * 2 * ROWS * TOK * D, bytes_accessed=9_000_000, transcendentals=2 * ROWS * TOK
        ),
    )(place, anchor_island, cot, gathered)


def swap(value, axis, mask):
    count = lax.axis_size(axis)
    return lax.ppermute(value, axis, [(i, i ^ mask) for i in range(count)])


def small_call(kernel, out_shapes, *args):
    vmem = pl.BlockSpec(memory_space=pltpu.VMEM)
    return pl.pallas_call(
        kernel,
        out_shape=[jax.ShapeDtypeStruct(shape, dtype) for shape, dtype in out_shapes],
        in_specs=[vmem] * len(args),
        out_specs=[vmem] * len(out_shapes),
        compiler_params=pltpu.CompilerParams(vmem_limit_bytes=8 * 1024 * 1024),
    )(*args)


def window_kernel(delta_hbm, sums_ref, sems):
    copies = [
        pltpu.make_async_copy(
            delta_hbm.at[0, :, pl.ds(i * (D // 4) // 128 * 128, WINDOW)], sums_ref.at[i], sems.at[i]
        )
        for i in range(4)
    ]
    for copy in copies:
        copy.start()
    for copy in copies:
        copy.wait()


def windows(prev_delta):
    return pl.pallas_call(
        window_kernel,
        out_shape=jax.ShapeDtypeStruct((4, ROWS, WINDOW), jnp.bfloat16),
        in_specs=[pl.BlockSpec(memory_space=pl.ANY)],
        out_specs=pl.BlockSpec(memory_space=pltpu.VMEM),
        scratch_shapes=[pltpu.SemaphoreType.DMA((4,))],
        compiler_params=pltpu.CompilerParams(vmem_limit_bytes=56 * 1024 * 1024),
    )(prev_delta)


def middle_kernel(place_ref, sums_ref, anchor_ref, out_ref):
    sums = sum(sums_ref[i].astype(jnp.float32) for i in range(4))
    sums = jnp.where(place_ref[1] % 2 == 1, sums[:, WINDOW - D // 4 :], sums[:, : D // 4])
    for i in range(4):
        out_ref[i, 0] = sums[:, i * WIDTH : (i + 1) * WIDTH].astype(jnp.bfloat16)
        out_ref[i, 1] = anchor_ref[...]


def square_kernel(mixed_ref, stale_ref, corrected_ref, out_ref):
    averaged = sum(mixed_ref[i, 0].astype(jnp.float32) for i in range(4)) / 16
    corrected = averaged + (PENALTY * averaged - stale_ref[...])
    corrected_ref[...] = corrected
    squares = jnp.sum(corrected * corrected, axis=(0, 1), keepdims=True)
    shape = (ROWS, WINDOW - D // 4)
    lane = lax.broadcasted_iota(jnp.int32, shape, 1)
    squares = jnp.broadcast_to(squares, shape)
    top = squares.astype(jnp.bfloat16).astype(jnp.float32)
    middle = (squares - top).astype(jnp.bfloat16).astype(jnp.float32)
    note = jnp.where(lane == 0, top, jnp.where(lane == 1, middle, squares - top - middle))
    note = jnp.where(lane < 3, note, 0.0).astype(jnp.bfloat16)
    for j in range(4):
        block = mixed_ref[j, 1]
        for i in range(4):
            out_ref[i, :, j * WIDTH : (j + 1) * WIDTH] = block
    for i in range(4):
        out_ref[i, :, D // 4 :] = note


def unpack_kernel(blocks_ref, anchor_ref, spread_ref):
    shape = (ROWS, 128)
    lane = lax.broadcasted_iota(jnp.int32, shape, 1)
    row = lax.broadcasted_iota(jnp.int32, shape, 0)
    squares = jnp.zeros(shape, jnp.float32)
    for i in range(4):
        anchor_ref[:, i * (D // 4) : (i + 1) * (D // 4)] = blocks_ref[i, :, : D // 4]
        squares = squares + blocks_ref[i, :, WINDOW - 128 :].astype(jnp.float32)
    squares = jnp.where((row == 0) & (lane >= 128 - (WINDOW - D // 4)), squares, 0.0)
    squares = jnp.sum(squares, axis=(0, 1), keepdims=True)
    spread_ref[...] = jnp.broadcast_to(squares.reshape(1, 1, 1), spread_ref.shape)


def outer_kernel(spread_ref, corrected_ref, momentum_ref, anchor_ref, new_anchor_ref, new_momentum_ref):
    squares = jnp.sum(spread_ref[...], axis=0)[:, :1]
    max_norm = CLIP_SHARE * math.sqrt(D * HW)
    factor = jnp.minimum(1.0, max_norm / jnp.sqrt(squares + 1e-06))
    clipped = factor * corrected_ref[...]
    new_momentum = MOMENT_DECAY * momentum_ref[...] + clipped
    new_momentum_ref[...] = new_momentum
    new_anchor_ref[...] = anchor_ref[...] - OUTER_RATE * (MOMENT_DECAY * new_momentum + clipped)


def middle(place, sums, rounded):
    vmem = pl.BlockSpec(memory_space=pltpu.VMEM)
    return pl.pallas_call(
        middle_kernel,
        out_shape=[jax.ShapeDtypeStruct((4, 2, ROWS, WIDTH), jnp.bfloat16)],
        in_specs=[pl.BlockSpec(memory_space=pltpu.SMEM), vmem, vmem],
        out_specs=[vmem],
        compiler_params=pltpu.CompilerParams(vmem_limit_bytes=8 * 1024 * 1024),
        cost_estimate=pl.CostEstimate(flops=200000000000, bytes_accessed=1_000_000, transcendentals=0),
    )(place, sums, rounded)


def body(anchor, prev_delta, momentum, pool, ids, cotangent):
    tie = lax.optimization_barrier
    bf16, f32 = jnp.bfloat16, jnp.float32
    block = (ROWS, WIDTH)
    place = jnp.stack([lax.axis_index("zl"), lax.axis_index("x")]).astype(jnp.int32)
    sampled = jnp.pad(ids[0].T, ((0, 0), (0, EXT - ids.shape[1]))).astype(bf16)
    rows = jnp.concatenate([pool[0], sampled], axis=1)
    other_rows = swap(rows, "zl", 1)
    sums = windows(prev_delta)
    pairs, held_anchor, held_momentum = tie((jnp.stack([rows, other_rows]), anchor, momentum))
    gathered = lax.all_gather(pairs, ("y", "c"), axis=0)
    rounded = held_anchor.astype(bf16)
    stale = PENALTY * held_momentum

    sums = lax.all_to_all(sums, "x", 0, 0)
    sums, rounded, stale = tie((sums, rounded, stale))
    (mixed,) = middle(place, sums, rounded)
    mixed = lax.all_to_all(mixed, "zh", 0, 0)
    corrected, blocks = small_call(
        square_kernel, [(block, f32), ((4, ROWS, WINDOW), bf16)], mixed, stale
    )
    blocks = lax.all_to_all(blocks, "x", 0, 0)
    anchor_island, spread = small_call(
        unpack_kernel, [((ROWS, D), bf16), ((128, 1, 128), f32)], blocks
    )
    spread = lax.all_to_all(spread, ("zh", *FSDP), 0, 0)
    new_delta = inner_steps(place, anchor_island, cotangent[0], gathered)
    spread, new_delta = tie((spread, new_delta))
    new_anchor, new_momentum = small_call(
        outer_kernel, [(block, f32), (block, f32)], spread, corrected, momentum, anchor
    )
    return (new_delta[None], new_anchor, new_momentum)


def solution(mesh):
    fine = Mesh(mesh.devices.reshape(4, 4, 2, 8, 2), REPLICA + FSDP)
    return jax.shard_map(
        body,
        mesh=fine,
        in_specs=(
            P(FSDP, REPLICA),
            P(REPLICA, FSDP, None),
            P(FSDP, REPLICA),
            P(REPLICA, FSDP, None),
            P(REPLICA, None, FSDP),
            P(REPLICA, None, FSDP, None),
        ),
        out_specs=(P(REPLICA, FSDP, None), P(FSDP, REPLICA), P(FSDP, REPLICA)),
        check_vma=False,
    )
```

```python
import math

import jax
import jax.numpy as jnp
from jax import lax
from jax.experimental import pallas as pl
from jax.experimental.pallas import tpu as pltpu
from jax.sharding import Mesh
from jax.sharding import PartitionSpec as P

D = 3328
HW = 3328
TOK = 1024
ROWS = 104
BLOCK = 32
EXT = 128
CHUNK = 256
COLS = 256
WIDTH = D // 16
WINDOW = 896

INNER_RATE = 2.0
INNER_DECAY = 0.1
PENALTY = 0.5
MOMENT_DECAY = 0.9
OUTER_RATE = 0.7
CLIP_SHARE = 0.05

FSDP = ("zl", "y", "c")
REPLICA = ("x", "zh")


def silu_slope(preact):
    sigmoid_val = jax.nn.sigmoid(preact)
    return sigmoid_val * (1.0 + preact * (1.0 - sigmoid_val))


def inner_kernel(
    place_ref, anchor_ref, cot_ref, pool_hbm, delta_ref, pool, weights, rounded, folded, sems
):
    copies = []
    for zl in range(2):
        for half in range(2):
            rows = pl.ds(half * 8, 8)
            copy = pltpu.make_async_copy(
                pool_hbm.at[rows, zl ^ place_ref[0]], pool.at[zl, rows], sems.at[zl * 2 + half]
            )
            copy.start()
            copies.append(copy)
    root_width = math.sqrt(D)

    def picks(chunk, step):
        part = pool[chunk // 2, (chunk % 2) * 8 : (chunk % 2) * 8 + 8, :, D:]
        ids = part.reshape(CHUNK, EXT)[:, step : step + 1].astype(jnp.float32).astype(jnp.int32)
        token = lax.broadcasted_iota(jnp.int32, (CHUNK, CHUNK), 0)
        row = lax.broadcasted_iota(jnp.int32, (CHUNK, CHUNK), 1)
        return jnp.where(row == (token // BLOCK) * BLOCK + ids, 1.0, 0.0).astype(jnp.bfloat16)

    def project(chunk, step):
        if step == 0:
            copies[chunk].wait()
        left = anchor_ref[...] if step == 0 else rounded[...]
        block = pool[chunk // 2, (chunk % 2) * 8 : (chunk % 2) * 8 + 8, :, :D].reshape(CHUNK, D)
        return lax.dot_general(
            left, block, (((1,), (1,)), ((), ())), preferred_element_type=jnp.float32
        )

    def fold(chunk, step, values):
        picked = picks(chunk, step)
        tokens = slice(chunk * CHUNK, (chunk + 1) * CHUNK)
        preact = jnp.zeros((ROWS, CHUNK), jnp.float32)
        for _ in range(2):
            top = values.astype(jnp.bfloat16)
            values = values - top.astype(jnp.float32)
            preact = preact + lax.dot_general(
                top, picked, (((1,), (1,)), ((), ())), preferred_element_type=jnp.float32
            )
        preact = preact / root_width
        scaled = cot_ref[step, :, tokens].astype(jnp.float32) * silu_slope(preact)
        folded[:, tokens] = jnp.dot(
            scaled.astype(jnp.bfloat16), picked, preferred_element_type=jnp.float32
        ).astype(jnp.bfloat16)

    for step in range(2):
        values = project(0, step)
        for chunk in range(1, TOK // CHUNK):
            later = project(chunk, step)
            fold(chunk - 1, step, values)
            values = later
        fold(TOK // CHUNK - 1, step, values)
        for start in range(0, D, COLS):
            cols = slice(start, start + COLS)
            tile = pool[:, :, :, cols].reshape(TOK, COLS)
            if start == 0:
                early = TOK - CHUNK
                gradient = jnp.dot(
                    folded[:, :early], tile[:early], preferred_element_type=jnp.float32
                ) + jnp.dot(folded[:, early:], tile[early:], preferred_element_type=jnp.float32)
            else:
                gradient = jnp.dot(folded[...], tile, preferred_element_type=jnp.float32)
            before = anchor_ref[:, cols].astype(jnp.float32)
            if step == 0:
                after = before - INNER_RATE * (gradient / root_width) - INNER_DECAY * before
                weights[:, cols] = after
                rounded[:, cols] = after.astype(jnp.bfloat16)
            else:
                last = weights[:, cols]
                after = last - INNER_RATE * (gradient / root_width) - INNER_DECAY * last
                delta_ref[:, cols] = (before - after).astype(jnp.bfloat16)


def inner_steps(place, anchor_island, cot, gathered):
    vmem = pl.BlockSpec(memory_space=pltpu.VMEM)
    return pl.pallas_call(
        inner_kernel,
        out_shape=jax.ShapeDtypeStruct((ROWS, D), jnp.bfloat16),
        in_specs=[
            pl.BlockSpec(memory_space=pltpu.SMEM),
            vmem,
            vmem,
            pl.BlockSpec(memory_space=pl.ANY),
        ],
        out_specs=vmem,
        scratch_shapes=[
            pltpu.VMEM((2, 16, BLOCK, D + EXT), jnp.bfloat16),
            pltpu.VMEM((ROWS, D), jnp.float32),
            pltpu.VMEM((ROWS, D), jnp.bfloat16),
            pltpu.VMEM((ROWS, TOK), jnp.bfloat16),
            pltpu.SemaphoreType.DMA((4,)),
        ],
        compiler_params=pltpu.CompilerParams(vmem_limit_bytes=50 * 1024 * 1024),
        cost_estimate=pl.CostEstimate(
            flops=4 * 2 * ROWS * TOK * D, bytes_accessed=9_000_000, transcendentals=2 * ROWS * TOK
        ),
    )(place, anchor_island, cot, gathered)


def swap(value, axis, mask):
    count = lax.axis_size(axis)
    return lax.ppermute(value, axis, [(i, i ^ mask) for i in range(count)])


def small_call(kernel, out_shapes, *args):
    vmem = pl.BlockSpec(memory_space=pltpu.VMEM)
    return pl.pallas_call(
        kernel,
        out_shape=[jax.ShapeDtypeStruct(shape, dtype) for shape, dtype in out_shapes],
        in_specs=[vmem] * len(args),
        out_specs=[vmem] * len(out_shapes),
        compiler_params=pltpu.CompilerParams(vmem_limit_bytes=8 * 1024 * 1024),
    )(*args)


def window_kernel(delta_hbm, sums_ref, sems):
    copies = [
        pltpu.make_async_copy(
            delta_hbm.at[0, :, pl.ds(i * (D // 4) // 128 * 128, WINDOW)], sums_ref.at[i], sems.at[i]
        )
        for i in range(4)
    ]
    for copy in copies:
        copy.start()
    for copy in copies:
        copy.wait()


def windows(prev_delta):
    return pl.pallas_call(
        window_kernel,
        out_shape=jax.ShapeDtypeStruct((4, ROWS, WINDOW), jnp.bfloat16),
        in_specs=[pl.BlockSpec(memory_space=pl.ANY)],
        out_specs=pl.BlockSpec(memory_space=pltpu.VMEM),
        scratch_shapes=[pltpu.SemaphoreType.DMA((4,))],
        compiler_params=pltpu.CompilerParams(vmem_limit_bytes=56 * 1024 * 1024),
    )(prev_delta)


def middle_kernel(place_ref, sums_ref, anchor_ref, out_ref):
    sums = sum(sums_ref[i].astype(jnp.float32) for i in range(4))
    sums = jnp.where(place_ref[1] % 2 == 1, sums[:, WINDOW - D // 4 :], sums[:, : D // 4])
    for i in range(4):
        out_ref[i, 0] = sums[:, i * WIDTH : (i + 1) * WIDTH].astype(jnp.bfloat16)
        out_ref[i, 1] = anchor_ref[...]


def square_kernel(mixed_ref, stale_ref, corrected_ref, out_ref):
    averaged = sum(mixed_ref[i, 0].astype(jnp.float32) for i in range(4)) / 16
    corrected = averaged + (PENALTY * averaged - stale_ref[...])
    corrected_ref[...] = corrected
    squares = jnp.sum(corrected * corrected, axis=(0, 1), keepdims=True)
    shape = (ROWS, WINDOW - D // 4)
    lane = lax.broadcasted_iota(jnp.int32, shape, 1)
    squares = jnp.broadcast_to(squares, shape)
    top = squares.astype(jnp.bfloat16).astype(jnp.float32)
    middle = (squares - top).astype(jnp.bfloat16).astype(jnp.float32)
    note = jnp.where(lane == 0, top, jnp.where(lane == 1, middle, squares - top - middle))
    note = jnp.where(lane < 3, note, 0.0).astype(jnp.bfloat16)
    for j in range(4):
        block = mixed_ref[j, 1]
        for i in range(4):
            out_ref[i, :, j * WIDTH : (j + 1) * WIDTH] = block
    for i in range(4):
        out_ref[i, :, D // 4 :] = note


def unpack_kernel(blocks_ref, anchor_ref, spread_ref):
    shape = (ROWS, 128)
    lane = lax.broadcasted_iota(jnp.int32, shape, 1)
    row = lax.broadcasted_iota(jnp.int32, shape, 0)
    squares = jnp.zeros(shape, jnp.float32)
    for i in range(4):
        anchor_ref[:, i * (D // 4) : (i + 1) * (D // 4)] = blocks_ref[i, :, : D // 4]
        squares = squares + blocks_ref[i, :, WINDOW - 128 :].astype(jnp.float32)
    squares = jnp.where((row == 0) & (lane >= 128 - (WINDOW - D // 4)), squares, 0.0)
    squares = jnp.sum(squares, axis=(0, 1), keepdims=True)
    spread_ref[...] = jnp.broadcast_to(squares.reshape(1, 1, 1), spread_ref.shape)


def outer_kernel(spread_ref, corrected_ref, momentum_ref, anchor_ref, new_anchor_ref, new_momentum_ref):
    squares = jnp.sum(spread_ref[...], axis=0)[:, :1]
    max_norm = CLIP_SHARE * math.sqrt(D * HW)
    factor = jnp.minimum(1.0, max_norm / jnp.sqrt(squares + 1e-06))
    clipped = factor * corrected_ref[...]
    new_momentum = MOMENT_DECAY * momentum_ref[...] + clipped
    new_momentum_ref[...] = new_momentum
    new_anchor_ref[...] = anchor_ref[...] - OUTER_RATE * (MOMENT_DECAY * new_momentum + clipped)


def middle(place, sums, rounded):
    vmem = pl.BlockSpec(memory_space=pltpu.VMEM)
    return pl.pallas_call(
        middle_kernel,
        out_shape=[jax.ShapeDtypeStruct((4, 2, ROWS, WIDTH), jnp.bfloat16)],
        in_specs=[pl.BlockSpec(memory_space=pltpu.SMEM), vmem, vmem],
        out_specs=[vmem],
        compiler_params=pltpu.CompilerParams(vmem_limit_bytes=8 * 1024 * 1024),
        cost_estimate=pl.CostEstimate(flops=200000000000, bytes_accessed=1_000_000, transcendentals=0),
    )(place, sums, rounded)


def body(anchor, prev_delta, momentum, pool, ids, cotangent):
    tie = lax.optimization_barrier
    bf16, f32 = jnp.bfloat16, jnp.float32
    block = (ROWS, WIDTH)
    place = jnp.stack([lax.axis_index("zl"), lax.axis_index("x")]).astype(jnp.int32)
    sampled = jnp.pad(ids[0].T, ((0, 0), (0, EXT - ids.shape[1]))).astype(bf16)
    rows = jnp.concatenate([pool[0], sampled], axis=1)
    other_rows = swap(rows, "zl", 1)
    sums = windows(prev_delta)
    pairs, held_anchor, held_momentum = tie((jnp.stack([rows, other_rows]), anchor, momentum))
    gathered = lax.all_gather(pairs, ("y", "c"), axis=0)
    rounded = held_anchor.astype(bf16)
    stale = PENALTY * held_momentum

    sums = lax.all_to_all(sums, "x", 0, 0)
    sums, rounded, stale = tie((sums, rounded, stale))
    (mixed,) = middle(place, sums, rounded)
    mixed = lax.all_to_all(mixed, "zh", 0, 0)
    corrected, blocks = small_call(
        square_kernel, [(block, f32), ((4, ROWS, WINDOW), bf16)], mixed, stale
    )
    blocks = lax.all_to_all(blocks, "x", 0, 0)
    anchor_island, spread = small_call(
        unpack_kernel, [((ROWS, D), bf16), ((128, 1, 128), f32)], blocks
    )
    spread = lax.all_to_all(spread, ("zh", *FSDP), 0, 0)
    new_delta = inner_steps(place, anchor_island, cotangent[0], gathered)
    spread, new_delta = tie((spread, new_delta))
    new_anchor, new_momentum = small_call(
        outer_kernel, [(block, f32), (block, f32)], spread, corrected, momentum, anchor
    )
    return (new_delta[None], new_anchor, new_momentum)


def solution(mesh):
    fine = Mesh(mesh.devices.reshape(4, 4, 2, 8, 2), REPLICA + FSDP)
    return jax.shard_map(
        body,
        mesh=fine,
        in_specs=(
            P(FSDP, REPLICA),
            P(REPLICA, FSDP, None),
            P(FSDP, REPLICA),
            P(REPLICA, FSDP, None),
            P(REPLICA, None, FSDP),
            P(REPLICA, None, FSDP, None),
        ),
        out_specs=(P(REPLICA, FSDP, None), P(FSDP, REPLICA), P(FSDP, REPLICA)),
        check_vma=False,
    )
```
